512 devices in a mesh: frames: 16 (over y_hi, x, core), tiles: 32 (over y_lo, z).
Axes of the slice: x: 4, y: 8 (y_hi: 2, y_lo: 4; y = y_hi * 4 + y_lo), z: 8, core: 2. Of those that a mesh axis runs over, the one named last changes fastest.
Arguments:
- queries: bfloat16 [2, 32, 512, 3072], P(None, 'frames', 'tiles'), may hold values from -10 to 10
- keys: bfloat16 [2, 32, 512, 3072], P(None, 'frames', 'tiles'), may hold values from -4 to 4
- values: bfloat16 [2, 32, 512, 3072], P(None, 'frames', 'tiles'), may hold values from -6 to 6
- segment_ids: int32 [2, 32], replicated, may hold values from 0 to 15, never falling along the last dimension, each value on 1 to 3 neighbouring positions
Outputs:
- normed: bfloat16 [2, 32, 512, 3072], P(None, 'frames', 'tiles')
The draws below stay inside these ranges and needn't reach their ends.
Inputs may be any that keep to these rules, and one draw needn't show every extreme that they name: `segment_ids`: non-decreasing along the frames of a clip, starting at 0 and rising by 0 or 1 from frame to frame; every value covers 1 to 3 consecutive frames.
All inputs are finite; a program needn't handle non-finite values.
Results may differ from the reference program's by a relative error of at most 0.012.
Values may be sent and summed in bfloat16 or wider, within the bound.
A program may use at most 128 MiB of HBM per device.

```python
import math
import jax
import jax.numpy as jnp
import numpy as np
from jax import lax

HEADS = 32
HD = 96
TOK_FRAME = 512
CLIPS = 2
D = 3072
FRAMES = 32


def draw_queries(key, part):
    key = jax.random.fold_in(key, 11)
    shape = (CLIPS, FRAMES, TOK_FRAME, HEADS * HD)
    base = jnp.clip(jax.random.normal(key, shape, jnp.float32), -4.0, 4.0)
    return base.astype(jnp.bfloat16)


def draw_keys(key, part):
    key = jax.random.fold_in(key, 12)
    shape = (CLIPS, FRAMES, TOK_FRAME, HEADS * HD)
    base = jnp.clip(jax.random.normal(key, shape, jnp.float32), -4.0, 4.0)
    return base.astype(jnp.bfloat16)


def levels(own_key, shape, split, low, top_value):
    def one(dim, shards_of):
        heights = jax.random.uniform(jax.random.fold_in(jax.random.fold_in(own_key, 6), dim), (shards_of,), jnp.float32, low / len(split), top_value / len(split))
        return jnp.repeat(jnp.exp(heights), shape[dim] // shards_of).reshape((-1,) + (1,) * (len(shape) - dim - 1))

    gain = one(*split[0])
    for cut in split[1:]:
        gain = gain * one(*cut)
    return gain


def profile(amount, total, bound, slope):
    loads = [(1 << 20) // math.isqrt(rank ** slope) + 1 for rank in range(2, amount + 1)]
    spare, holding = total - bound - (amount - 1), [1] * (amount - 1)
    while spare > 0:
        movable = [i for i in range(amount - 1) if holding[i] < bound]
        pool, budget = sum([loads[i] for i in movable]), spare
        for i in movable:
            addition = min(bound - holding[i], max(1, budget * loads[i] // pool), spare)
            holding[i] = holding[i] + addition
            spare = spare - addition
    return np.array([bound] + holding)


def uneven_parts(key, count, total, reach, skew):
    if count == 2:
        one = jax.random.randint(key, (), max(1, total - reach), min(reach, total - 1) + 1)
        return jnp.stack([one, total - one])
    tallies = jnp.asarray(profile(count, total, reach, skew), jnp.int32)
    twos = (count - 1) // 2
    source_of, sink = tallies[1:1 + 2 * twos:2], tallies[2:2 + 2 * twos:2]
    slack = jnp.minimum(source_of - 1, reach - sink)
    shifted = jax.random.randint(jax.random.fold_in(key, 1), (twos,), 0, 1 << 20) % (slack + 1)
    tallies = tallies.at[1:1 + 2 * twos:2].set(source_of - shifted).at[2:2 + 2 * twos:2].set(sink + shifted)
    return tallies[jax.random.permutation(jax.random.fold_in(key, 2), count)]


def bell_draw(stream_key, dims, spread, most, shards=(), kind=jnp.bfloat16):
    loudness = levels(stream_key, dims, shards, -0.22, 0.18) if shards else 1.0
    result = jax.random.normal(stream_key, dims, jnp.float32) * spread * loudness
    return jnp.minimum(jnp.maximum(result, -most), most).astype(kind)


def setup_inputs(seed: int = 0) -> dict:
    splits = jax.random.split(jax.random.key(seed), 5)
    queries = draw_queries(jax.random.fold_in(splits[4], 71), 0)
    keys = draw_keys(jax.random.fold_in(splits[4], 71), 0)
    values = bell_draw(splits[2], (CLIPS, FRAMES, TOK_FRAME, D), 1.0, 6.0, ((1, 16), (2, 32)))
    segment_ids = jax.vmap(lambda own: jnp.searchsorted(jnp.cumsum(uneven_parts(own, FRAMES // 2, FRAMES, 3, 0)), jnp.arange(FRAMES), side="right"))(jax.random.split(splits[3], CLIPS)).reshape((CLIPS, FRAMES)).astype(jnp.int32)
    return dict(queries=queries, keys=keys, values=values, segment_ids=segment_ids)


floor_score = -1e+30

def reference(queries, keys, values, segment_ids):
    scale_factor = HD ** (-0.5)

    def one_frame(flat_index):
        clip_index = flat_index // FRAMES
        query_frame = flat_index % FRAMES
        clip_queries = lax.dynamic_index_in_dim(queries, clip_index, 0, keepdims=False)
        frame_queries = lax.dynamic_index_in_dim(clip_queries, query_frame, 0, keepdims=False)
        frame_queries = frame_queries.reshape(TOK_FRAME, HEADS, HD).astype(jnp.float32)
        clip_keys = lax.dynamic_index_in_dim(keys, clip_index, 0, keepdims=False)
        clip_values = lax.dynamic_index_in_dim(values, clip_index, 0, keepdims=False)
        clip_ids = lax.dynamic_index_in_dim(segment_ids, clip_index, 0, keepdims=False)
        query_id = lax.dynamic_index_in_dim(clip_ids, query_frame, 0, keepdims=False)

        def visit_frame(carried, key_frame):

            def update(previous):
                running_max, totals, summed_values = previous
                frame_keys = lax.dynamic_index_in_dim(clip_keys, key_frame, 0, keepdims=False)
                frame_keys = frame_keys.reshape(TOK_FRAME, HEADS, HD).astype(jnp.float32)
                frame_values = lax.dynamic_index_in_dim(clip_values, key_frame, 0, keepdims=False)
                frame_values = frame_values.reshape(TOK_FRAME, HEADS, HD).astype(jnp.float32)
                scores = jnp.einsum('qhd,khd->hqk', frame_queries, frame_keys) * scale_factor
                newest_max = jnp.maximum(running_max, lax.optimization_barrier(jnp.max(scores, axis=-1)))
                weights = jnp.exp(scores - newest_max[..., None])
                rescale = jnp.exp(running_max - newest_max)
                totals = totals * rescale + lax.optimization_barrier(jnp.sum(weights, axis=-1))
                rounded = lax.optimization_barrier(weights.astype(jnp.bfloat16)).astype(jnp.float32)
                increment = jnp.einsum('hqk,khd->hqd', rounded, frame_values)
                return (newest_max, totals, summed_values * rescale[..., None] + increment)

            def keep_state(previous):
                return previous
            key_id = lax.dynamic_index_in_dim(clip_ids, key_frame, 0, keepdims=False)
            return (lax.cond(key_id <= query_id, update, keep_state, carried), None)
        start_state = (jnp.full((HEADS, TOK_FRAME), floor_score, jnp.float32), jnp.zeros((HEADS, TOK_FRAME), jnp.float32), jnp.zeros((HEADS, TOK_FRAME, HD), jnp.float32))
        final_state, unused = lax.scan(visit_frame, start_state, jnp.arange(FRAMES, dtype=jnp.int32))
        context = (final_state[2] / final_state[1][..., None]).astype(jnp.bfloat16)
        context = jnp.transpose(context, (1, 0, 2)).reshape(TOK_FRAME, HEADS * HD)
        context_wide = lax.optimization_barrier(context).astype(jnp.float32)
        inverse_rms = lax.rsqrt(lax.optimization_barrier(jnp.mean(context_wide * context_wide, axis=-1, keepdims=True)) + 1e-06)
        return (context_wide * inverse_rms).astype(jnp.bfloat16)
    normed = lax.map(one_frame, jnp.arange(CLIPS * FRAMES, dtype=jnp.int32))
    return normed.reshape(CLIPS, FRAMES, TOK_FRAME, HEADS * HD)
```

```python
import functools
import math

import jax
import jax.numpy as jnp
from jax import lax
from jax.experimental import pallas as pl
from jax.experimental.pallas import tpu as pltpu
from jax.sharding import PartitionSpec as P

MESH = pl.DeviceIdType.MESH
HD = 96
CLIPS = 2
NX, NCORE, NZ = 4, 2, 8
YH, YL = 2, 4
ND = NX * NCORE
GROUP = YL * HD
TOK = 16
RUN = NZ * TOK
FRAME_TOK = YL * RUN
NF = 2
FRAMES = YH * ND * NF
SCALE2 = HD ** (-0.5) * math.log2(math.e)
NF_Q = YH * NF
DEPTH = 256
LOW = -1e30
NT = (((1,), (1,)), ((), ()))


def place():
    fi = lax.axis_index("frames")
    ti = lax.axis_index("tiles")
    yh, d = fi // ND, fi % ND
    return yh, d, ti // NZ, ti % NZ


def dev(yh, d, yl, z):
    return (yh * ND + d, yl * NZ + z)


def greet(targets_of):
    barrier = pltpu.get_barrier_semaphore()
    total = 0
    for count, target in targets_of:
        total += count

        def one(k, carry, target=target):
            pl.semaphore_signal(barrier, inc=1, device_id=target(k), device_id_type=MESH)
            return carry

        lax.fori_loop(0, count, one, 0)
    pl.semaphore_wait(barrier, total)


def remote(src, dst, send, recv, target):
    return pltpu.make_async_remote_copy(
        src_ref=src, dst_ref=dst, send_sem=send, recv_sem=recv, device_id=target, device_id_type=MESH
    )


def kernel(
    seg, k_in, v_in, q_in, out, k_all, v_all, q_own, tokens, turned, rows_q, acc, top, scores, heads, feats, spun, rows,
    a_send, a_recv, b_send, b_recv, c_send, c_recv, d_send, d_recv, e_send, e_recv
):
    yh, d, yl, z = place()
    y = yh * YL + yl
    x, core = d // NCORE, d % NCORE
    up = lax.rem(x + 1, NX) * NCORE + core
    down = lax.rem(x + NX - 1, NX) * NCORE + core
    far = lax.rem(x + 2, NX) * NCORE + core
    twin = x * NCORE + 1 - core
    mirror = ND - 1 - d

    def z_peer(k):
        return lax.rem(z + 1 + k, NZ)

    def y_peer(k):
        yy = lax.rem(y + 1 + k, YH * YL)
        return yy // YL, lax.rem(yy, YL)

    greet(
        [
            (NZ - 1, lambda k: dev(yh, d, yl, z_peer(k))),
            (YH * YL - 1, lambda k: dev(y_peer(k)[0], d, y_peer(k)[1], z)),
            (YH * YL, lambda k: dev(k // YL, mirror, lax.rem(k, YL), z)),
            (1, lambda k: dev(yh, up, yl, z)),
            (1, lambda k: dev(yh, down, yl, z)),
            (1, lambda k: dev(yh, twin, yl, z)),
        ]
    )

    inputs = (k_in, v_in, q_in)
    chunks = [(0, 0), (1, 0), (2, 0), (2, 1), (0, 1), (1, 1)]
    key0, value0, query0, query1, key1, value1 = range(6)

    def a_src(t, zz):
        tensor, f = chunks[t]
        return inputs[tensor].at[:, f, :, pl.ds(pl.multiple_of(zz * GROUP, 128), GROUP)]

    def a_dst(t, zz):
        return tokens.at[t, :, pl.ds(pl.multiple_of(zz * TOK, TOK), TOK), :]

    def a_copy(t, k):
        zz = z_peer(k)
        return remote(a_src(t, zz), a_dst(t, z), a_send.at[t, zz], a_recv.at[t, z], dev(yh, d, yl, zz))

    def a_start(t):
        def one(k, carry):
            a_copy(t, k).start()
            return carry

        lax.fori_loop(0, NZ - 1, one, 0)
        pltpu.make_async_copy(a_src(t, z), a_dst(t, z), a_recv.at[t, z]).start()

    def a_wait(t):
        def one(zz, carry):
            pltpu.make_async_copy(a_src(t, zz), a_dst(t, zz), a_recv.at[t, zz]).wait()
            return carry

        lax.fori_loop(0, NZ, one, 0)

    def a_drain(t):
        def one(k, carry):
            a_copy(t, k).wait_send()
            return carry

        lax.fori_loop(0, NZ - 1, one, 0)

    def b_src(t, ch, hl):
        return turned.at[t, ch, pl.ds(pl.multiple_of(hl * HD, 32), HD), :]

    def b_dst(t, holder, h, l):
        tensor, f = chunks[t]
        lanes = pl.ds(pl.multiple_of(l * RUN, 128), RUN)
        if tensor == 2:
            return q_own.at[h, f, :, lanes]
        return (k_all, v_all)[tensor].at[h, holder, f, :, lanes]

    def b_copy(t, ch, hl, holder):
        return remote(
            b_src(t, ch, hl), b_dst(t, holder, yh, yl), b_send.at[t, ch * YL + hl], b_recv.at[t, y], dev(ch, holder, hl, z)
        )

    def b_start(t):
        for ch in range(CLIPS):
            turned[t, ch] = tokens[t, ch].T

        def one(k, carry):
            ch, hl = y_peer(k)
            if chunks[t][0] == 2:

                @pl.when(yh == 0)
                def _():
                    b_copy(t, ch, hl, d).start()

                @pl.when(yh == 1)
                def _():
                    b_copy(t, ch, hl, mirror).start()
            else:
                b_copy(t, ch, hl, d).start()
            return carry

        lax.fori_loop(0, YH * YL - 1, one, 0)
        own = pltpu.make_async_copy(b_src(t, yh, yl), b_dst(t, d, yh, yl), b_recv.at[t, y])
        if chunks[t][0] == 2:

            @pl.when(yh == 0)
            def _():
                own.start()

            @pl.when(yh == 1)
            def _():
                b_copy(t, yh, yl, mirror).start()
        else:
            own.start()

    def b_wait(t):
        def one(ys, carry):
            h, l = ys // YL, lax.rem(ys, YL)
            pltpu.make_async_copy(b_src(t, h, l), b_dst(t, d, h, l), b_recv.at[t, ys]).wait()
            return carry

        lax.fori_loop(0, YH * YL, one, 0)

    def b_drain(t):
        def one(k, carry):
            ch, hl = y_peer(k)
            b_copy(t, ch, hl, d).wait_send()
            return carry

        lax.fori_loop(0, YH * YL - 1, one, 0)
        if chunks[t][0] == 2:

            @pl.when(yh == 1)
            def _():
                b_copy(t, yh, yl, mirror).wait_send()

    def whole(t, holder):
        tensor, f = chunks[t]
        return (k_all, v_all)[tensor].at[:, holder, f]

    def half(t, holder, h):
        tensor, f = chunks[t]
        return (k_all, v_all)[tensor].at[h, holder, f]

    def c_copy(t, kind):
        ref, there = {
            0: (lambda: whole(t, d), up),
            1: (lambda: whole(t, d), down),
            2: (lambda: half(t, down, 0), up),
            3: (lambda: half(t, up, 1), down),
            4: (lambda: whole(t, d), twin),
            5: (lambda: whole(t, down), twin),
            6: (lambda: whole(t, up), twin),
            7: (lambda: half(t, far, 0), twin),
            8: (lambda: half(t, far, 1), twin),
        }[kind]
        ref = ref()
        return remote(ref, ref, c_send.at[t, kind], c_recv.at[t, kind], dev(yh, there, yl, z))

    def c_arrived(t, kind):
        far_twin = lax.rem(x + 2, NX) * NCORE + 1 - core
        up_twin = lax.rem(x + 1, NX) * NCORE + 1 - core
        down_twin = lax.rem(x + NX - 1, NX) * NCORE + 1 - core
        ref = {
            0: lambda: whole(t, down),
            1: lambda: whole(t, up),
            2: lambda: half(t, far, 0),
            3: lambda: half(t, far, 1),
            4: lambda: whole(t, twin),
            5: lambda: whole(t, down_twin),
            6: lambda: whole(t, up_twin),
            7: lambda: half(t, far_twin, 0),
            8: lambda: half(t, far_twin, 1),
        }[kind]()
        pltpu.make_async_copy(ref, ref, c_recv.at[t, kind]).wait()

    def c_start(t):
        b_wait(t)
        for kind in (0, 1, 4):
            c_copy(t, kind).start()

    def c_relay(t):
        c_arrived(t, 0)
        c_copy(t, 2).start()
        c_copy(t, 5).start()
        c_arrived(t, 1)
        c_copy(t, 3).start()
        c_copy(t, 6).start()

    def c_last(t):
        for kind in (2, 3):
            c_arrived(t, kind)
            c_copy(t, kind + 5).start()

    def c_end(t):
        for kind in range(9):
            c_copy(t, kind).wait_send()

    def query_frame(i):
        h, f = i // NF, i % NF
        return jnp.where(h == 0, d, YH * ND - 1 - d) * NF + f

    def prepare():
        spare = lax.broadcasted_iota(jnp.int32, (DEPTH - 2 * HD, FRAME_TOK), 0)
        flag = jnp.where(spare == 0, 1.0, 0.0).astype(jnp.bfloat16)
        for i in range(NF_Q):
            scaled = q_own[i // NF, i % NF].astype(jnp.float32) * SCALE2
            high = scaled.astype(jnp.bfloat16)
            low = (scaled - high.astype(jnp.float32)).astype(jnp.bfloat16)
            rows_q[i] = jnp.concatenate([high, low, flag], axis=0).T
            acc[i] = jnp.zeros(acc.shape[1:], jnp.float32)
            top[i] = jnp.full(top.shape[1:], LOW, jnp.float32)

    ones = jnp.ones((128 - HD, FRAME_TOK), jnp.bfloat16)
    spare_row = lax.broadcasted_iota(jnp.int32, (DEPTH - 2 * HD, FRAME_TOK), 0)

    def unit(i, h, xs, f):
        own_id = seg[yh, query_frame(i)]
        highest = None
        for c in range(NCORE):
            holder = xs * NCORE + c
            bias = jnp.where(seg[yh, (h * ND + holder) * NF + f] <= own_id, 0.0, LOW)
            block = k_all[h, holder, f]
            extra = jnp.where(spare_row == 0, bias, 0.0).astype(jnp.bfloat16)
            s = jnp.dot(
                rows_q[i], jnp.concatenate([block, block, extra], axis=0), preferred_element_type=jnp.float32
            )
            scores[c] = s
            for lane in range(0, FRAME_TOK, 128):
                part = s[:, lane : lane + 128]
                highest = part if highest is None else jnp.maximum(highest, part)
        before = top[i]
        newest = jnp.maximum(before, jnp.max(highest, axis=1, keepdims=True))
        top[i] = newest
        wide = jnp.concatenate([newest] * (FRAME_TOK // 128), axis=1)
        total = acc[i] * jnp.exp2(before - newest)
        for c in range(NCORE):
            p = jnp.exp2(scores[c] - wide).astype(jnp.bfloat16)
            block = jnp.concatenate([v_all[h, xs * NCORE + c, f], ones], axis=0)
            total += lax.dot_general(p, block, NT, preferred_element_type=jnp.float32)
        acc[i] = total

    def visit(xs, f):
        def one(n, carry):
            h, i = n // NF_Q, lax.rem(n, NF_Q)

            @pl.when((h * ND + xs * NCORE) * NF + f <= query_frame(i) + 2)
            def _():
                unit(i, h, xs, f)

            return carry

        lax.fori_loop(0, YH * NF_Q, one, 0)

    def sweep(i, f, first, last):
        def one(n, carry):
            unit(i, n // NX, lax.rem(n, NX), f)
            return carry

        seen = (query_frame(i) + 2 - f) // (NCORE * NF) + 1
        lax.fori_loop(first, jnp.minimum(seen, last), one, 0)

    def d_src(i, l):
        return heads.at[i, :, pl.ds(pl.multiple_of(l * RUN, 128), RUN)]

    def d_dst(f, clip, hl):
        return feats.at[f, clip, pl.ds(pl.multiple_of(hl * HD, 32), HD), :]

    def d_copy(i, l):
        h, f = i // NF, i % NF
        there = d if h == 0 else mirror
        return remote(d_src(i, l), d_dst(f, yh, yl), d_send.at[i, l], d_recv.at[f, y], dev(h, there, l, z))

    def d_run(i, act):
        def one(k, carry):
            act(d_copy(i, lax.rem(yl + 1 + k, YL)))
            return carry

        lax.fori_loop(0, YL - 1, one, 0)

    def d_start(i):
        total = acc[i]
        heads[i] = (total[:, :HD] / total[:, HD : HD + 1]).astype(jnp.bfloat16).T
        d_run(i, lambda copy: copy.start())
        if i < NF:

            @pl.when(yh == 0)
            def _():
                pltpu.make_async_copy(d_src(i, yl), d_dst(i, yh, yl), d_recv.at[i, y]).start()

            @pl.when(yh == 1)
            def _():
                d_copy(i, yl).start()
        else:
            d_copy(i, yl).start()

    def d_wait(f):
        def one(ys, carry):
            c, l = ys // YL, lax.rem(ys, YL)
            pltpu.make_async_copy(d_src(f, l), d_dst(f, c, l), d_recv.at[f, ys]).wait()
            return carry

        lax.fori_loop(0, YH * YL, one, 0)

    def d_drain(i):
        d_run(i, lambda copy: copy.wait_send())
        if i < NF:

            @pl.when(yh == 1)
            def _():
                d_copy(i, yl).wait_send()
        else:
            d_copy(i, yl).wait_send()

    def e_src(f, zz):
        return spun.at[f, :, pl.ds(pl.multiple_of(zz * TOK, TOK), TOK), :]

    def e_dst(f, zz):
        return rows.at[:, f, :, pl.ds(pl.multiple_of(zz * GROUP, 128), GROUP)]

    def e_copy(f, k):
        zz = z_peer(k)
        return remote(e_src(f, zz), e_dst(f, z), e_send.at[f, zz], e_recv.at[f, z], dev(yh, d, yl, zz))

    def e_run(f, act):
        def one(k, carry):
            act(e_copy(f, k))
            return carry

        lax.fori_loop(0, NZ - 1, one, 0)

    def e_start(f):
        d_wait(f)
        for clip in range(CLIPS):
            spun[f, clip] = feats[f, clip].T
        pltpu.make_async_copy(e_src(f, z), e_dst(f, z), e_recv.at[f, z]).start()
        e_run(f, lambda copy: copy.start())

    def e_finish(f):
        def one(zz, carry):
            pltpu.make_async_copy(e_src(f, zz), e_dst(f, zz), e_recv.at[f, zz]).wait()
            return carry

        lax.fori_loop(0, NZ, one, 0)
        for clip in range(CLIPS):
            context = rows[clip, f].astype(jnp.float32)
            inverse_rms = lax.rsqrt(jnp.mean(context * context, axis=-1, keepdims=True) + 1e-06)
            out[clip, f] = (context * inverse_rms).astype(jnp.bfloat16)

    for t in range(6):
        a_start(t)
    a_wait(key0)
    b_start(key0)
    a_wait(value0)
    b_start(value0)
    c_start(key0)
    a_wait(query0)
    b_start(query0)
    c_start(value0)
    a_wait(query1)
    b_start(query1)
    c_relay(key0)
    a_wait(key1)
    b_start(key1)
    c_relay(value0)
    a_wait(value1)
    b_start(value1)
    b_wait(query0)
    b_wait(query1)
    prepare()
    x_up, x_down, x_far = lax.rem(x + 1, NX), lax.rem(x + NX - 1, NX), lax.rem(x + 2, NX)

    def ready(f, kinds):
        for t in ((key0, value0), (key1, value1))[f]:
            for kind in kinds:
                c_arrived(t, kind)

    c_start(key1)
    c_last(key0)
    ready(0, (4,))
    visit(x, 0)
    c_start(value1)
    c_last(value0)
    ready(0, (5,))
    visit(x_down, 0)
    c_relay(key1)
    ready(0, (6,))
    visit(x_up, 0)
    c_relay(value1)
    c_last(key1)
    ready(0, (7, 8))
    visit(x_far, 0)
    c_last(value1)
    ready(1, (4, 5, 6, 7, 8))
    for i in range(NF_Q - 1):
        sweep(i, 1, 0, YH * NX)
        d_start(i)
    sweep(NF_Q - 1, 1, 0, 4)
    e_start(0)
    sweep(NF_Q - 1, 1, 4, YH * NX)
    d_start(NF_Q - 1)
    e_start(1)
    e_finish(0)
    e_finish(1)
    for t in range(6):
        a_drain(t)
        b_drain(t)
        if chunks[t][0] < 2:
            c_end(t)
    for i in range(NF_Q):
        d_drain(i)
    for f in range(NF):
        e_run(f, lambda copy: copy.wait_send())


def on_device(queries, keys, values, segment_ids):
    hbm = pl.BlockSpec(memory_space=pltpu.HBM)
    vmem = pl.BlockSpec(memory_space=pltpu.VMEM)
    gathered = pltpu.VMEM((YH, ND, NF, HD, FRAME_TOK), jnp.bfloat16)
    state = pltpu.VMEM((NF_Q, FRAME_TOK, 128), jnp.float32)
    dma = pltpu.SemaphoreType.DMA
    return pl.pallas_call(
        kernel,
        out_shape=jax.ShapeDtypeStruct((CLIPS, NF, TOK, NZ * GROUP), jnp.bfloat16),
        in_specs=[pl.BlockSpec(memory_space=pltpu.SMEM), hbm, hbm, hbm],
        out_specs=vmem,
        scratch_shapes=[
            gathered,
            gathered,
            pltpu.VMEM((YH, NF, HD, FRAME_TOK), jnp.bfloat16),
            pltpu.VMEM((6, CLIPS, RUN, GROUP), jnp.bfloat16),
            pltpu.VMEM((6, CLIPS, GROUP, RUN), jnp.bfloat16),
            pltpu.VMEM((NF_Q, FRAME_TOK, DEPTH), jnp.bfloat16),
            state,
            state,
            pltpu.VMEM((NCORE, FRAME_TOK, FRAME_TOK), jnp.float32),
            pltpu.VMEM((NF_Q, HD, FRAME_TOK), jnp.bfloat16),
            pltpu.VMEM((NF, CLIPS, GROUP, RUN), jnp.bfloat16),
            pltpu.VMEM((NF, CLIPS, RUN, GROUP), jnp.bfloat16),
            pltpu.VMEM((CLIPS, NF, TOK, NZ * GROUP), jnp.bfloat16),
            dma((6, NZ)),
            dma((6, NZ)),
            dma((6, YH * YL)),
            dma((6, YH * YL)),
            dma((6, 9)),
            dma((6, 9)),
            dma((NF_Q, YL)),
            dma((NF, YH * YL)),
            dma((NF, NZ)),
            dma((NF, NZ)),
        ],
        compiler_params=pltpu.CompilerParams(collective_id=0, has_side_effects=True, vmem_limit_bytes=56 << 20),
        name="attend",
    )(segment_ids, keys, values, queries)


def solution(mesh):
    rows = P(None, "frames", "tiles", None)
    return jax.shard_map(
        on_device,
        mesh=mesh,
        in_specs=(rows, rows, rows, P()),
        out_specs=rows,
        check_vma=False,
    )
```

```python
import functools
import math

import jax
import jax.numpy as jnp
from jax import lax
from jax.experimental import pallas as pl
from jax.experimental.pallas import tpu as pltpu
from jax.sharding import PartitionSpec as P

MESH = pl.DeviceIdType.MESH
HD = 96
CLIPS = 2
NX, NCORE, NZ = 4, 2, 8
YH, YL = 2, 4
ND = NX * NCORE
GROUP = YL * HD
TOK = 16
RUN = NZ * TOK
FRAME_TOK = YL * RUN
NF = 2
FRAMES = YH * ND * NF
SCALE2 = HD ** (-0.5) * math.log2(math.e)
NF_Q = YH * NF
DEPTH = 256
LOW = -1e30
NT = (((1,), (1,)), ((), ()))


def place():
    fi = lax.axis_index("frames")
    ti = lax.axis_index("tiles")
    yh, d = fi // ND, fi % ND
    return yh, d, ti // NZ, ti % NZ


def dev(yh, d, yl, z):
    return (yh * ND + d, yl * NZ + z)


def greet(targets_of):
    barrier = pltpu.get_barrier_semaphore()
    total = 0
    for count, target in targets_of:
        total += count

        def one(k, carry, target=target):
            pl.semaphore_signal(barrier, inc=1, device_id=target(k), device_id_type=MESH)
            return carry

        lax.fori_loop(0, count, one, 0)
    pl.semaphore_wait(barrier, total)


def remote(src, dst, send, recv, target):
    return pltpu.make_async_remote_copy(
        src_ref=src, dst_ref=dst, send_sem=send, recv_sem=recv, device_id=target, device_id_type=MESH
    )


def kernel(
    seg, k_in, v_in, q_in, out, k_all, v_all, q_own, tokens, turned, rows_q, acc, top, scores, heads, feats, spun, rows,
    a_send, a_recv, b_send, b_recv, c_send, c_recv, d_send, d_recv, e_send, e_recv
):
    yh, d, yl, z = place()
    y = yh * YL + yl
    x, core = d // NCORE, d % NCORE
    up = lax.rem(x + 1, NX) * NCORE + core
    down = lax.rem(x + NX - 1, NX) * NCORE + core
    far = lax.rem(x + 2, NX) * NCORE + core
    twin = x * NCORE + 1 - core
    mirror = ND - 1 - d

    def z_peer(k):
        return lax.rem(z + 1 + k, NZ)

    def y_peer(k):
        yy = lax.rem(y + 1 + k, YH * YL)
        return yy // YL, lax.rem(yy, YL)

    greet(
        [
            (NZ - 1, lambda k: dev(yh, d, yl, z_peer(k))),
            (YH * YL - 1, lambda k: dev(y_peer(k)[0], d, y_peer(k)[1], z)),
            (YH * YL, lambda k: dev(k // YL, mirror, lax.rem(k, YL), z)),
            (1, lambda k: dev(yh, up, yl, z)),
            (1, lambda k: dev(yh, down, yl, z)),
            (1, lambda k: dev(yh, twin, yl, z)),
        ]
    )

    inputs = (k_in, v_in, q_in)
    chunks = [(0, 0), (1, 0), (2, 0), (2, 1), (0, 1), (1, 1)]
    key0, value0, query0, query1, key1, value1 = range(6)

    def a_src(t, zz):
        tensor, f = chunks[t]
        return inputs[tensor].at[:, f, :, pl.ds(pl.multiple_of(zz * GROUP, 128), GROUP)]

    def a_dst(t, zz):
        return tokens.at[t, :, pl.ds(pl.multiple_of(zz * TOK, TOK), TOK), :]

    def a_copy(t, k):
        zz = z_peer(k)
        return remote(a_src(t, zz), a_dst(t, z), a_send.at[t, zz], a_recv.at[t, z], dev(yh, d, yl, zz))

    def a_start(t):
        def one(k, carry):
            a_copy(t, k).start()
            return carry

        lax.fori_loop(0, NZ - 1, one, 0)
        pltpu.make_async_copy(a_src(t, z), a_dst(t, z), a_recv.at[t, z]).start()

    def a_wait(t):
        def one(zz, carry):
            pltpu.make_async_copy(a_src(t, zz), a_dst(t, zz), a_recv.at[t, zz]).wait()
            return carry

        lax.fori_loop(0, NZ, one, 0)

    def a_drain(t):
        def one(k, carry):
            a_copy(t, k).wait_send()
            return carry

        lax.fori_loop(0, NZ - 1, one, 0)

    def b_src(t, ch, hl):
        return turned.at[t, ch, pl.ds(pl.multiple_of(hl * HD, 32), HD), :]

    def b_dst(t, holder, h, l):
        tensor, f = chunks[t]
        lanes = pl.ds(pl.multiple_of(l * RUN, 128), RUN)
        if tensor == 2:
            return q_own.at[h, f, :, lanes]
        return (k_all, v_all)[tensor].at[h, holder, f, :, lanes]

    def b_copy(t, ch, hl, holder):
        return remote(
            b_src(t, ch, hl), b_dst(t, holder, yh, yl), b_send.at[t, ch * YL + hl], b_recv.at[t, y], dev(ch, holder, hl, z)
        )

    def b_start(t):
        for ch in range(CLIPS):
            turned[t, ch] = tokens[t, ch].T

        def one(k, carry):
            ch, hl = y_peer(k)
            if chunks[t][0] == 2:

                @pl.when(yh == 0)
                def _():
                    b_copy(t, ch, hl, d).start()

                @pl.when(yh == 1)
                def _():
                    b_copy(t, ch, hl, mirror).start()
            else:
                b_copy(t, ch, hl, d).start()
            return carry

        lax.fori_loop(0, YH * YL - 1, one, 0)
        own = pltpu.make_async_copy(b_src(t, yh, yl), b_dst(t, d, yh, yl), b_recv.at[t, y])
        if chunks[t][0] == 2:

            @pl.when(yh == 0)
            def _():
                own.start()

            @pl.when(yh == 1)
            def _():
                b_copy(t, yh, yl, mirror).start()
        else:
            own.start()

    def b_wait(t):
        def one(ys, carry):
            h, l = ys // YL, lax.rem(ys, YL)
            pltpu.make_async_copy(b_src(t, h, l), b_dst(t, d, h, l), b_recv.at[t, ys]).wait()
            return carry

        lax.fori_loop(0, YH * YL, one, 0)

    def b_drain(t):
        def one(k, carry):
            ch, hl = y_peer(k)
            b_copy(t, ch, hl, d).wait_send()
            return carry

        lax.fori_loop(0, YH * YL - 1, one, 0)
        if chunks[t][0] == 2:

            @pl.when(yh == 1)
            def _():
                b_copy(t, yh, yl, mirror).wait_send()

    def whole(t, holder):
        tensor, f = chunks[t]
        return (k_all, v_all)[tensor].at[:, holder, f]

    def half(t, holder, h):
        tensor, f = chunks[t]
        return (k_all, v_all)[tensor].at[h, holder, f]

    def c_copy(t, kind):
        ref, there = {
            0: (lambda: whole(t, d), up),
            1: (lambda: whole(t, d), down),
            2: (lambda: half(t, down, 0), up),
            3: (lambda: half(t, up, 1), down),
            4: (lambda: whole(t, d), twin),
            5: (lambda: whole(t, down), twin),
            6: (lambda: whole(t, up), twin),
            7: (lambda: half(t, far, 0), twin),
            8: (lambda: half(t, far, 1), twin),
        }[kind]
        ref = ref()
        return remote(ref, ref, c_send.at[t, kind], c_recv.at[t, kind], dev(yh, there, yl, z))

    def c_arrived(t, kind):
        far_twin = lax.rem(x + 2, NX) * NCORE + 1 - core
        up_twin = lax.rem(x + 1, NX) * NCORE + 1 - core
        down_twin = lax.rem(x + NX - 1, NX) * NCORE + 1 - core
        ref = {
            0: lambda: whole(t, down),
            1: lambda: whole(t, up),
            2: lambda: half(t, far, 0),
            3: lambda: half(t, far, 1),
            4: lambda: whole(t, twin),
            5: lambda: whole(t, down_twin),
            6: lambda: whole(t, up_twin),
            7: lambda: half(t, far_twin, 0),
            8: lambda: half(t, far_twin, 1),
        }[kind]()
        pltpu.make_async_copy(ref, ref, c_recv.at[t, kind]).wait()

    def c_start(t):
        b_wait(t)
        for kind in (0, 1, 4):
            c_copy(t, kind).start()

    def c_relay(t):
        c_arrived(t, 0)
        c_copy(t, 2).start()
        c_copy(t, 5).start()
        c_arrived(t, 1)
        c_copy(t, 3).start()
        c_copy(t, 6).start()

    def c_last(t):
        for kind in (2, 3):
            c_arrived(t, kind)
            c_copy(t, kind + 5).start()

    def c_end(t):
        for kind in range(9):
            c_copy(t, kind).wait_send()

    def query_frame(i):
        h, f = i // NF, i % NF
        return jnp.where(h == 0, d, YH * ND - 1 - d) * NF + f

    def prepare():
        spare = lax.broadcasted_iota(jnp.int32, (DEPTH - 2 * HD, FRAME_TOK), 0)
        flag = jnp.where(spare == 0, 1.0, 0.0).astype(jnp.bfloat16)
        for i in range(NF_Q):
            scaled = q_own[i // NF, i % NF].astype(jnp.float32) * SCALE2
            high = scaled.astype(jnp.bfloat16)
            low = (scaled - high.astype(jnp.float32)).astype(jnp.bfloat16)
            rows_q[i] = jnp.concatenate([high, low, flag], axis=0).T
            acc[i] = jnp.zeros(acc.shape[1:], jnp.float32)
            top[i] = jnp.full(top.shape[1:], LOW, jnp.float32)

    ones = jnp.ones((128 - HD, FRAME_TOK), jnp.bfloat16)
    spare_row = lax.broadcasted_iota(jnp.int32, (DEPTH - 2 * HD, FRAME_TOK), 0)

    def score(i, h, xs, f, slot):
        own_id = seg[yh, query_frame(i)]
        for c in range(NCORE):
            holder = xs * NCORE + c
            bias = jnp.where(seg[yh, (h * ND + holder) * NF + f] <= own_id, 0.0, LOW)
            block = k_all[h, holder, f]
            extra = jnp.where(spare_row == 0, bias, 0.0).astype(jnp.bfloat16)
            block = jnp.concatenate([block, block, extra], axis=0)
            scores[slot, c] = jnp.dot(rows_q[i], block, preferred_element_type=jnp.float32)

    def weigh(i, h, xs, f, slot):
        highest = None
        for c in range(NCORE):
            for lane in range(0, FRAME_TOK, 128):
                part = scores[slot, c, :, lane : lane + 128]
                highest = part if highest is None else jnp.maximum(highest, part)
        before = top[i]
        newest = jnp.maximum(before, jnp.max(highest, axis=1, keepdims=True))
        top[i] = newest
        wide = jnp.concatenate([newest] * (FRAME_TOK // 128), axis=1)
        total = acc[i] * jnp.exp2(before - newest)
        for c in range(NCORE):
            p = jnp.exp2(scores[slot, c] - wide).astype(jnp.bfloat16)
            block = jnp.concatenate([v_all[h, xs * NCORE + c, f], ones], axis=0)
            total += lax.dot_general(p, block, NT, preferred_element_type=jnp.float32)
        acc[i] = total

    def visit(xs, f):
        def one(n, carry):
            h, pair = n // YH, lax.rem(n, YH)
            i = pair * NF

            @pl.when((h * ND + xs * NCORE) * NF + f <= query_frame(i + 1) + 2)
            def _():
                score(i, h, xs, f, 0)
                score(i + 1, h, xs, f, 1)
                weigh(i, h, xs, f, 0)
                weigh(i + 1, h, xs, f, 1)

            return carry

        lax.fori_loop(0, YH * YH, one, 0)

    def sweep(i, f, first, last):
        def one(n, carry):
            h, xs = n // (NX // 2), lax.rem(n, NX // 2) * 2
            score(i, h, xs, f, 0)
            score(i, h, xs + 1, f, 1)
            weigh(i, h, xs, f, 0)
            weigh(i, h, xs + 1, f, 1)
            return carry

        seen = (query_frame(i) + 2 - f) // (2 * NCORE * NF) + 1
        lax.fori_loop(first, jnp.minimum(seen, last), one, 0)

    def d_src(i, l):
        return heads.at[i, :, pl.ds(pl.multiple_of(l * RUN, 128), RUN)]

    def d_dst(f, clip, hl):
        return feats.at[f, clip, pl.ds(pl.multiple_of(hl * HD, 32), HD), :]

    def d_copy(i, l):
        h, f = i // NF, i % NF
        there = d if h == 0 else mirror
        return remote(d_src(i, l), d_dst(f, yh, yl), d_send.at[i, l], d_recv.at[f, y], dev(h, there, l, z))

    def d_run(i, act):
        def one(k, carry):
            act(d_copy(i, lax.rem(yl + 1 + k, YL)))
            return carry

        lax.fori_loop(0, YL - 1, one, 0)

    def d_start(i):
        total = acc[i]
        heads[i] = (total[:, :HD] / total[:, HD : HD + 1]).astype(jnp.bfloat16).T
        d_run(i, lambda copy: copy.start())
        if i < NF:

            @pl.when(yh == 0)
            def _():
                pltpu.make_async_copy(d_src(i, yl), d_dst(i, yh, yl), d_recv.at[i, y]).start()

            @pl.when(yh == 1)
            def _():
                d_copy(i, yl).start()
        else:
            d_copy(i, yl).start()

    def d_wait(f):
        def one(ys, carry):
            c, l = ys // YL, lax.rem(ys, YL)
            pltpu.make_async_copy(d_src(f, l), d_dst(f, c, l), d_recv.at[f, ys]).wait()
            return carry

        lax.fori_loop(0, YH * YL, one, 0)

    def d_drain(i):
        d_run(i, lambda copy: copy.wait_send())
        if i < NF:

            @pl.when(yh == 1)
            def _():
                d_copy(i, yl).wait_send()
        else:
            d_copy(i, yl).wait_send()

    def e_src(f, zz):
        return spun.at[f, :, pl.ds(pl.multiple_of(zz * TOK, TOK), TOK), :]

    def e_dst(f, zz):
        return rows.at[:, f, :, pl.ds(pl.multiple_of(zz * GROUP, 128), GROUP)]

    def e_copy(f, k):
        zz = z_peer(k)
        return remote(e_src(f, zz), e_dst(f, z), e_send.at[f, zz], e_recv.at[f, z], dev(yh, d, yl, zz))

    def e_run(f, act):
        def one(k, carry):
            act(e_copy(f, k))
            return carry

        lax.fori_loop(0, NZ - 1, one, 0)

    def e_start(f):
        d_wait(f)
        for clip in range(CLIPS):
            spun[f, clip] = feats[f, clip].T
        pltpu.make_async_copy(e_src(f, z), e_dst(f, z), e_recv.at[f, z]).start()
        e_run(f, lambda copy: copy.start())

    def e_finish(f):
        def one(zz, carry):
            pltpu.make_async_copy(e_src(f, zz), e_dst(f, zz), e_recv.at[f, zz]).wait()
            return carry

        lax.fori_loop(0, NZ, one, 0)
        for clip in range(CLIPS):
            context = rows[clip, f].astype(jnp.float32)
            inverse_rms = lax.rsqrt(jnp.mean(context * context, axis=-1, keepdims=True) + 1e-06)
            out[clip, f] = (context * inverse_rms).astype(jnp.bfloat16)

    for t in range(6):
        a_start(t)
    a_wait(key0)
    b_start(key0)
    a_wait(value0)
    b_start(value0)
    c_start(key0)
    a_wait(query0)
    b_start(query0)
    c_start(value0)
    a_wait(query1)
    b_start(query1)
    c_relay(key0)
    a_wait(key1)
    b_start(key1)
    c_relay(value0)
    a_wait(value1)
    b_start(value1)
    b_wait(query0)
    b_wait(query1)
    prepare()
    x_up, x_down, x_far = lax.rem(x + 1, NX), lax.rem(x + NX - 1, NX), lax.rem(x + 2, NX)

    def ready(f, kinds):
        for t in ((key0, value0), (key1, value1))[f]:
            for kind in kinds:
                c_arrived(t, kind)

    c_start(key1)
    c_last(key0)
    ready(0, (4,))
    visit(x, 0)
    c_start(value1)
    c_last(value0)
    ready(0, (5,))
    visit(x_down, 0)
    c_relay(key1)
    ready(0, (6,))
    visit(x_up, 0)
    c_relay(value1)
    c_last(key1)
    ready(0, (7, 8))
    visit(x_far, 0)
    c_last(value1)
    ready(1, (4, 5, 6, 7, 8))
    for i in range(NF_Q - 1):
        sweep(i, 1, 0, YH * NX // 2)
        d_start(i)
    sweep(NF_Q - 1, 1, 0, 2)
    e_start(0)
    sweep(NF_Q - 1, 1, 2, YH * NX // 2)
    d_start(NF_Q - 1)
    e_start(1)
    e_finish(0)
    e_finish(1)
    for t in range(6):
        a_drain(t)
        b_drain(t)
        if chunks[t][0] < 2:
            c_end(t)
    for i in range(NF_Q):
        d_drain(i)
    for f in range(NF):
        e_run(f, lambda copy: copy.wait_send())


def on_device(queries, keys, values, segment_ids):
    hbm = pl.BlockSpec(memory_space=pltpu.HBM)
    vmem = pl.BlockSpec(memory_space=pltpu.VMEM)
    gathered = pltpu.VMEM((YH, ND, NF, HD, FRAME_TOK), jnp.bfloat16)
    state = pltpu.VMEM((NF_Q, FRAME_TOK, 128), jnp.float32)
    dma = pltpu.SemaphoreType.DMA
    return pl.pallas_call(
        kernel,
        out_shape=jax.ShapeDtypeStruct((CLIPS, NF, TOK, NZ * GROUP), jnp.bfloat16),
        in_specs=[pl.BlockSpec(memory_space=pltpu.SMEM), hbm, hbm, hbm],
        out_specs=vmem,
        scratch_shapes=[
            gathered,
            gathered,
            pltpu.VMEM((YH, NF, HD, FRAME_TOK), jnp.bfloat16),
            pltpu.VMEM((6, CLIPS, RUN, GROUP), jnp.bfloat16),
            pltpu.VMEM((6, CLIPS, GROUP, RUN), jnp.bfloat16),
            pltpu.VMEM((NF_Q, FRAME_TOK, DEPTH), jnp.bfloat16),
            state,
            state,
            pltpu.VMEM((2, NCORE, FRAME_TOK, FRAME_TOK), jnp.float32),
            pltpu.VMEM((NF_Q, HD, FRAME_TOK), jnp.bfloat16),
            pltpu.VMEM((NF, CLIPS, GROUP, RUN), jnp.bfloat16),
            pltpu.VMEM((NF, CLIPS, RUN, GROUP), jnp.bfloat16),
            pltpu.VMEM((CLIPS, NF, TOK, NZ * GROUP), jnp.bfloat16),
            dma((6, NZ)),
            dma((6, NZ)),
            dma((6, YH * YL)),
            dma((6, YH * YL)),
            dma((6, 9)),
            dma((6, 9)),
            dma((NF_Q, YL)),
            dma((NF, YH * YL)),
            dma((NF, NZ)),
            dma((NF, NZ)),
        ],
        compiler_params=pltpu.CompilerParams(collective_id=0, has_side_effects=True, vmem_limit_bytes=56 << 20),
        name="attend",
    )(segment_ids, keys, values, queries)


def solution(mesh):
    rows = P(None, "frames", "tiles", None)
    return jax.shard_map(
        on_device,
        mesh=mesh,
        in_specs=(rows, rows, rows, P()),
        out_specs=rows,
        check_vma=False,
    )
```

```python
import functools
import math

import jax
import jax.numpy as jnp
from jax import lax
from jax.experimental import pallas as pl
from jax.experimental.pallas import tpu as pltpu
from jax.sharding import PartitionSpec as P

MESH = pl.DeviceIdType.MESH
HD = 96
CLIPS = 2
NX, NCORE, NZ = 4, 2, 8
YH, YL = 2, 4
ND = NX * NCORE
GROUP = YL * HD
TOK = 16
RUN = NZ * TOK
FRAME_TOK = YL * RUN
NF = 2
FRAMES = YH * ND * NF
SCALE2 = HD ** (-0.5) * math.log2(math.e)
NF_Q = YH * NF
DEPTH = 256
LOW = -1e30
NT = (((1,), (1,)), ((), ()))


def place():
    fi = lax.axis_index("frames")
    ti = lax.axis_index("tiles")
    yh, d = fi // ND, fi % ND
    return yh, d, ti // NZ, ti % NZ


def dev(yh, d, yl, z):
    return (yh * ND + d, yl * NZ + z)


def greet(partners):
    barrier = pltpu.get_barrier_semaphore()
    for partner in partners:
        pl.semaphore_signal(barrier, inc=1, device_id=partner, device_id_type=MESH)
    pl.semaphore_wait(barrier, len(partners))


def take(ref, semaphore):
    pltpu.make_async_copy(ref, ref, semaphore).wait()


def remote(src, dst, send, recv, target):
    return pltpu.make_async_remote_copy(
        src_ref=src, dst_ref=dst, send_sem=send, recv_sem=recv, device_id=target, device_id_type=MESH
    )


def kernel(
    seg, k_in, v_in, q_in, out, k_all, v_all, q_own, tokens, tokens_q, turned, turned_q, rows_q, acc, top, scores,
    heads, feats, spun, rows, a_send, a_recv, b_send, b_recv, c_send, c_recv, d_send, d_recv, e_send, e_recv
):
    yh, d, yl, z = place()
    y = yh * YL + yl
    x, core = d // NCORE, d % NCORE
    up = lax.rem(x + 1, NX) * NCORE + core
    down = lax.rem(x + NX - 1, NX) * NCORE + core
    far = lax.rem(x + 2, NX) * NCORE + core
    twin = x * NCORE + 1 - core
    mirror = ND - 1 - d
    z_peers = [lax.rem(z + k, NZ) for k in range(1, NZ)]
    y_peers = [(yy // YL, lax.rem(yy, YL)) for yy in [lax.rem(y + k, YH * YL) for k in range(1, YH * YL)]]

    greet(
        [dev(yh, d, yl, zz) for zz in z_peers]
        + [dev(h, d, l, z) for h, l in y_peers]
        + [dev(h, mirror, l, z) for h in range(YH) for l in range(YL)]
        + [dev(yh, there, yl, z) for there in (up, down, twin)]
    )

    key0, value0, query, key1, value1 = range(5)
    arrays = (k_all, v_all, None, k_all, v_all)
    inputs = (k_in, v_in, q_in, k_in, v_in)
    frame_of = (0, 0, None, 1, 1)

    def a_src(t, zz):
        lanes = pl.ds(pl.multiple_of(zz * GROUP, 128), GROUP)
        if t == query:
            return q_in.at[:, :, :, lanes]
        return inputs[t].at[:, frame_of[t], :, lanes]

    def a_dst(t, first, count):
        run = pl.ds(pl.multiple_of(first, TOK), count)
        if t == query:
            return tokens_q.at[:, :, run, :]
        return tokens.at[t, :, run, :]

    def a_start(t):
        mine = a_dst(t, z * TOK, TOK)
        for zz in z_peers:
            remote(a_src(t, zz), mine, a_send.at[t], a_recv.at[t], dev(yh, d, yl, zz)).start()
        pltpu.make_async_copy(a_src(t, z), mine, a_recv.at[t]).start()

    def a_wait(t):
        take(a_dst(t, 0, RUN), a_recv.at[t])

    def a_drain(t):
        take(a_dst(t, 0, RUN - TOK), a_send.at[t])

    def b_src(t, first, count):
        run = pl.ds(pl.multiple_of(first, 32), count)
        if t == query:
            return turned_q.at[:, run, :]
        return turned.at[t, run, :]

    def b_dst(t, h, l):
        lanes = pl.ds(pl.multiple_of(l * RUN, 128), RUN)
        if t == query:
            return q_own.at[h, :, :, lanes]
        return arrays[t].at[h, d, frame_of[t], :, lanes]

    def b_copy(t, h, l, holder):
        block = b_src(t, (h * YL + l) * HD, HD)
        return remote(block, b_dst(t, yh, yl), b_send.at[t], b_recv.at[t], dev(h, holder, l, z))

    def b_start(t):
        own = pltpu.make_async_copy(b_src(t, y * HD, HD), b_dst(t, yh, yl), b_recv.at[t])
        for clip in range(CLIPS):
            part = slice(clip * GROUP, (clip + 1) * GROUP)
            if t == query:
                for f in range(NF):
                    turned_q[f, part] = tokens_q[clip, f].T
            else:
                turned[t, part] = tokens[t, clip].T
        if t == query:

            @pl.when(yh == 0)
            def _():
                for h, l in y_peers:
                    b_copy(t, h, l, d).start()
                own.start()

            @pl.when(yh == 1)
            def _():
                for h, l in y_peers:
                    b_copy(t, h, l, mirror).start()
                b_copy(t, yh, yl, mirror).start()
        else:
            for h, l in y_peers:
                b_copy(t, h, l, d).start()
            own.start()

    def b_wait(t):
        take(q_own if t == query else whole(t, d), b_recv.at[t])

    def b_drain(t):
        most, every = CLIPS * GROUP - HD, CLIPS * GROUP
        if t == query:

            @pl.when(yh == 0)
            def _():
                take(b_src(t, 0, most), b_send.at[t])

            @pl.when(yh == 1)
            def _():
                take(b_src(t, 0, every), b_send.at[t])
        else:
            take(b_src(t, 0, most), b_send.at[t])

    def whole(t, holder):
        return arrays[t].at[:, holder, frame_of[t]]

    def half(t, holder, h):
        return arrays[t].at[h, holder, frame_of[t]]

    def c_copy(t, kind, ref, there):
        remote(ref, ref, c_send.at[t], c_recv.at[t, kind], dev(yh, there, yl, z)).start()

    def c_start(t):
        b_wait(t)
        c_copy(t, 0, whole(t, d), up)
        c_copy(t, 1, whole(t, d), down)
        c_copy(t, 4, whole(t, d), twin)

    def c_relay(t):
        take(whole(t, down), c_recv.at[t, 0])
        c_copy(t, 2, half(t, down, 0), up)
        c_copy(t, 5, whole(t, down), twin)
        take(whole(t, up), c_recv.at[t, 1])
        c_copy(t, 3, half(t, up, 1), down)
        c_copy(t, 6, whole(t, up), twin)

    def c_last(t):
        take(half(t, far, 0), c_recv.at[t, 2])
        c_copy(t, 7, half(t, far, 0), twin)
        take(half(t, far, 1), c_recv.at[t, 3])
        c_copy(t, 7, half(t, far, 1), twin)

    def c_ready(f, kind):
        for t in ((key0, value0), (key1, value1))[f]:
            take(whole(t, twin), c_recv.at[t, kind])

    def c_drain(t):
        take(arrays[t].at[:, pl.ds(0, 7), frame_of[t]], c_send.at[t])

    def query_frame(i):
        h, f = i // NF, i % NF
        return jnp.where(h == 0, d, YH * ND - 1 - d) * NF + f

    def prepare():
        spare = lax.broadcasted_iota(jnp.int32, (DEPTH - 2 * HD, FRAME_TOK), 0)
        flag = jnp.where(spare == 0, 1.0, 0.0).astype(jnp.bfloat16)
        for i in range(NF_Q):
            scaled = q_own[i // NF, i % NF].astype(jnp.float32) * SCALE2
            high = scaled.astype(jnp.bfloat16)
            low = (scaled - high.astype(jnp.float32)).astype(jnp.bfloat16)
            rows_q[i] = jnp.concatenate([high, low, flag], axis=0).T
            acc[i] = jnp.zeros(acc.shape[1:], jnp.float32)
            top[i] = jnp.full(top.shape[1:], LOW, jnp.float32)

    ones = jnp.ones((128 - HD, FRAME_TOK), jnp.bfloat16)
    spare_row = lax.broadcasted_iota(jnp.int32, (DEPTH - 2 * HD, FRAME_TOK), 0)

    def score(i, h, xs, f, slot):
        own_id = seg[yh, query_frame(i)]
        for c in range(NCORE):
            holder = xs * NCORE + c
            bias = jnp.where(seg[yh, (h * ND + holder) * NF + f] <= own_id, 0.0, LOW)
            block = k_all[h, holder, f]
            extra = jnp.where(spare_row == 0, bias, 0.0).astype(jnp.bfloat16)
            block = jnp.concatenate([block, block, extra], axis=0)
            scores[slot, c] = jnp.dot(rows_q[i], block, preferred_element_type=jnp.float32)

    def weigh(i, h, xs, f, slot):
        highest = None
        for c in range(NCORE):
            for lane in range(0, FRAME_TOK, 128):
                part = scores[slot, c, :, lane : lane + 128]
                highest = part if highest is None else jnp.maximum(highest, part)
        before = top[i]
        newest = jnp.maximum(before, jnp.max(highest, axis=1, keepdims=True))
        top[i] = newest
        wide = jnp.concatenate([newest] * (FRAME_TOK // 128), axis=1)
        total = acc[i] * jnp.exp2(before - newest)
        for c in range(NCORE):
            p = jnp.exp2(scores[slot, c] - wide).astype(jnp.bfloat16)
            block = jnp.concatenate([v_all[h, xs * NCORE + c, f], ones], axis=0)
            total += lax.dot_general(p, block, NT, preferred_element_type=jnp.float32)
        acc[i] = total

    def visit(xs, f):
        def one(n, carry):
            h, i = lax.rem(n, YH), n // YH * NF

            @pl.when((h * ND + xs * NCORE) * NF + f <= query_frame(i + 1) + 2)
            def _():
                score(i, h, xs, f, 0)
                score(i + 1, h, xs, f, 1)
                weigh(i, h, xs, f, 0)
                weigh(i + 1, h, xs, f, 1)

            return carry

        lax.fori_loop(0, YH * YH, one, 0)

    def sweep(i, f, first, last):
        def one(n, carry):
            h, xs = n // (NX // 2), lax.rem(n, NX // 2) * 2
            score(i, h, xs, f, 0)
            score(i, h, xs + 1, f, 1)
            weigh(i, h, xs, f, 0)
            weigh(i, h, xs + 1, f, 1)
            return carry

        seen = (query_frame(i) + 2 - f) // (2 * NCORE * NF) + 1
        lax.fori_loop(first, jnp.minimum(seen, last), one, 0)

    def d_src(i, first, count):
        return heads.at[i, :, pl.ds(pl.multiple_of(first, 128), count)]

    def d_copy(i, l):
        h, f = i // NF, i % NF
        there = d if h == 0 else mirror
        block = feats.at[f, yh, pl.ds(pl.multiple_of(yl * HD, 32), HD), :]
        return remote(d_src(i, l * RUN, RUN), block, d_send.at[i], d_recv.at[f], dev(h, there, l, z))

    def d_start(i):
        total = acc[i]
        heads[i] = (total[:, :HD] / total[:, HD : HD + 1]).astype(jnp.bfloat16).T
        for k in range(1, YL):
            d_copy(i, lax.rem(yl + k, YL)).start()
        if i < NF:

            @pl.when(yh == 0)
            def _():
                block = feats.at[i, yh, pl.ds(pl.multiple_of(yl * HD, 32), HD), :]
                pltpu.make_async_copy(d_src(i, yl * RUN, RUN), block, d_recv.at[i]).start()

            @pl.when(yh == 1)
            def _():
                d_copy(i, yl).start()
        else:
            d_copy(i, yl).start()

    def d_drain(i):
        if i < NF:

            @pl.when(yh == 0)
            def _():
                take(d_src(i, 0, FRAME_TOK - RUN), d_send.at[i])

            @pl.when(yh == 1)
            def _():
                take(d_src(i, 0, FRAME_TOK), d_send.at[i])
        else:
            take(d_src(i, 0, FRAME_TOK), d_send.at[i])

    def e_src(f, first, count):
        return spun.at[f, :, pl.ds(pl.multiple_of(first, TOK), count), :]

    def e_start(f):
        take(feats.at[f], d_recv.at[f])
        for clip in range(CLIPS):
            spun[f, clip] = feats[f, clip].T
        mine = rows.at[:, f, :, pl.ds(pl.multiple_of(z * GROUP, 128), GROUP)]
        for zz in z_peers:
            remote(e_src(f, zz * TOK, TOK), mine, e_send.at[f], e_recv.at[f], dev(yh, d, yl, zz)).start()
        pltpu.make_async_copy(e_src(f, z * TOK, TOK), mine, e_recv.at[f]).start()

    def e_finish(f):
        take(rows.at[:, f], e_recv.at[f])
        for clip in range(CLIPS):
            context = rows[clip, f].astype(jnp.float32)
            inverse_rms = lax.rsqrt(jnp.mean(context * context, axis=-1, keepdims=True) + 1e-06)
            out[clip, f] = (context * inverse_rms).astype(jnp.bfloat16)

    for t in range(5):
        a_start(t)
    a_wait(key0)
    b_start(key0)
    a_wait(value0)
    b_start(value0)
    c_start(key0)
    a_wait(query)
    b_start(query)
    c_start(value0)
    c_relay(key0)
    a_wait(key1)
    b_start(key1)
    c_relay(value0)
    a_wait(value1)
    b_start(value1)
    b_wait(query)
    prepare()
    c_start(key1)
    c_last(key0)
    c_ready(0, 4)
    visit(x, 0)
    c_start(value1)
    c_last(value0)
    c_ready(0, 5)
    visit(lax.rem(x + NX - 1, NX), 0)
    c_relay(key1)
    c_ready(0, 6)
    visit(lax.rem(x + 1, NX), 0)
    c_relay(value1)
    c_last(key1)
    c_ready(0, 7)
    visit(lax.rem(x + 2, NX), 0)
    for t in range(5):
        a_drain(t)
        b_drain(t)
    c_last(value1)
    for kind in (4, 5, 6, 7):
        c_ready(1, kind)
    for i in (0, 2, 1):
        sweep(i, 1, 0, YH * NX // 2)
        d_start(i)
    sweep(3, 1, 0, 2)
    e_start(0)
    sweep(3, 1, 2, YH * NX // 2)
    d_start(3)
    for t in (key0, value0, key1, value1):
        c_drain(t)
    e_start(1)
    for i in range(NF_Q):
        d_drain(i)
    e_finish(0)
    e_finish(1)
    for f in range(NF):
        take(e_src(f, 0, RUN - TOK), e_send.at[f])


def on_device(queries, keys, values, segment_ids):
    hbm = pl.BlockSpec(memory_space=pltpu.HBM)
    vmem = pl.BlockSpec(memory_space=pltpu.VMEM)
    gathered = pltpu.VMEM((YH, ND, NF, HD, FRAME_TOK), jnp.bfloat16)
    state = pltpu.VMEM((NF_Q, FRAME_TOK, 128), jnp.float32)
    dma = pltpu.SemaphoreType.DMA
    return pl.pallas_call(
        kernel,
        out_shape=jax.ShapeDtypeStruct((CLIPS, NF, TOK, NZ * GROUP), jnp.bfloat16),
        in_specs=[pl.BlockSpec(memory_space=pltpu.SMEM), hbm, hbm, hbm],
        out_specs=vmem,
        scratch_shapes=[
            gathered,
            gathered,
            pltpu.VMEM((YH, NF, HD, FRAME_TOK), jnp.bfloat16),
            pltpu.VMEM((5, CLIPS, RUN, GROUP), jnp.bfloat16),
            pltpu.VMEM((CLIPS, NF, RUN, GROUP), jnp.bfloat16),
            pltpu.VMEM((5, CLIPS * GROUP, RUN), jnp.bfloat16),
            pltpu.VMEM((NF, CLIPS * GROUP, RUN), jnp.bfloat16),
            pltpu.VMEM((NF_Q, FRAME_TOK, DEPTH), jnp.bfloat16),
            state,
            state,
            pltpu.VMEM((2, NCORE, FRAME_TOK, FRAME_TOK), jnp.float32),
            pltpu.VMEM((NF_Q, HD, FRAME_TOK), jnp.bfloat16),
            pltpu.VMEM((NF, CLIPS, GROUP, RUN), jnp.bfloat16),
            pltpu.VMEM((NF, CLIPS, RUN, GROUP), jnp.bfloat16),
            pltpu.VMEM((CLIPS, NF, TOK, NZ * GROUP), jnp.bfloat16),
            dma((5,)),
            dma((5,)),
            dma((5,)),
            dma((5,)),
            dma((5,)),
            dma((5, 8)),
            dma((NF_Q,)),
            dma((NF,)),
            dma((NF,)),
            dma((NF,)),
        ],
        compiler_params=pltpu.CompilerParams(collective_id=0, has_side_effects=True, vmem_limit_bytes=56 << 20),
        name="attend",
    )(segment_ids, keys, values, queries)


def solution(mesh):
    rows = P(None, "frames", "tiles", None)
    return jax.shard_map(
        on_device,
        mesh=mesh,
        in_specs=(rows, rows, rows, P()),
        out_specs=rows,
        check_vma=False,
    )
```
